32 devices in a mesh: site: 16 (over z, x, core), col: 2 (over y).
Axes of the slice: x: 2, y: 2, z: 4, core: 2. Of those that a mesh axis runs over, the one named last changes fastest.
Arguments:
- panel: bfloat16 [2, 32768, 1024], P(None, 'site', 'col'), may hold values from -0.03125 to 0.03125
- xs: int32 [32768], P(('site', 'col')), may hold values from 0 to 255, as said below
- ys: int32 [32768], P(('site', 'col')), may hold values from 0 to 127
Outputs:
- marker: float32 [32768], P(('site', 'col'))
The draws below stay inside these ranges and needn't reach their ends.
Inputs may be any that keep to these rules, and one draw needn't show every extreme that they name: The pairs (xs, ys) list every cell of a 256 by 128 lattice exactly once.
All inputs are finite; a program needn't handle non-finite values.
Results may differ from the reference program's by a relative error of at most 0.008.
Values may be sent and summed in bfloat16 or wider, within the bound.
A program may use at most 128 MiB of HBM per device.

```python
import math
import jax
import jax.numpy as jnp
from jax import lax

ROWS_DEV = 1024
K = 1024
LX = 256
SITES = 32768


def lattice_order(key):
    return jax.random.permutation(jax.random.fold_in(key, 11), SITES).astype(jnp.int32)


def draw_xs(key, part):
    return lattice_order(key) % LX


def draw_ys(key, part):
    return lattice_order(key) // LX


def level_of(rng, extent, split, low, largest):
    level = 1.0
    for axis_at, shards_of in split:
        steps = jax.random.uniform(jax.random.fold_in(jax.random.fold_in(rng, 6), axis_at), (shards_of,), jnp.float32, low / len(split), largest / len(split))
        level = level * jnp.repeat(jnp.exp(steps), extent[axis_at] // shards_of).reshape((-1,) + (1,) * (len(extent) - 1 - axis_at))
    return level


def bell_draw(key, extent, deviation, most, pieces=(), kind=jnp.bfloat16):
    result = deviation * jax.random.normal(key, extent, jnp.float32)
    if pieces:
        result = result * level_of(key, extent, pieces, -0.22, 0.18)
    return jnp.clip(result, -most, most).astype(kind)


def setup_inputs(seed: int = 0) -> dict:
    keys = jax.random.split(jax.random.key(seed), 4)
    panel = bell_draw(keys[0], (2, SITES, K), (1.0 / SITES ** 0.5), 0.03125, ((1, 16), (2, 2)))
    xs = draw_xs(jax.random.fold_in(keys[3], 71), 0)
    ys = draw_ys(jax.random.fold_in(keys[3], 71), 0)
    return {"panel": panel, "xs": xs, "ys": ys}


def product(first, second):
    return jnp.dot(first, second, preferred_element_type=jnp.float32)


def reference(panel, xs, ys):
    lat_y = SITES // LX
    centre_x = xs.astype(jnp.float32) - (LX - 1) / 2.0
    centre_y = ys.astype(jnp.float32) - (lat_y - 1) / 2.0
    blocks = SITES // ROWS_DEV
    slab_real = panel[0].reshape(blocks, ROWS_DEV, K)
    slab_imag = panel[1].reshape(blocks, ROWS_DEV, K)
    block_x = centre_x.reshape(blocks, ROWS_DEV)
    block_y = centre_y.reshape(blocks, ROWS_DEV)

    def gram_step(summed, items):
        real_rows, imag_rows, posx, posy = items
        xw_real = (posx[:, None] * real_rows).astype(jnp.bfloat16)
        xw_imag = (posx[:, None] * imag_rows).astype(jnp.bfloat16)
        yw_real = (posy[:, None] * real_rows).astype(jnp.bfloat16)
        yw_imag = (posy[:, None] * imag_rows).astype(jnp.bfloat16)
        part = jnp.concatenate([
            product(real_rows.T, xw_real) + product(imag_rows.T, xw_imag),
            product(real_rows.T, xw_imag) - product(imag_rows.T, xw_real),
            product(real_rows.T, yw_real) + product(imag_rows.T, yw_imag),
            product(real_rows.T, yw_imag) - product(imag_rows.T, yw_real)], axis=1)
        return summed + part, None

    summed, _ = lax.scan(gram_step, jnp.zeros((K, 4 * K), jnp.float32),
                         (slab_real, slab_imag, block_x, block_y))
    grams = summed.astype(jnp.bfloat16)
    gx_real = grams[:, :K]
    gx_imag = grams[:, K:2 * K]
    gy_real = grams[:, 2 * K:3 * K]
    gy_imag = grams[:, 3 * K:]
    comm_real = (product(gx_real, gy_real) - product(gx_imag, gy_imag)
                 - product(gy_real, gx_real) + product(gy_imag, gx_imag)).astype(jnp.bfloat16)
    comm_imag = (product(gx_real, gy_imag) + product(gx_imag, gy_real)
                 - product(gy_real, gx_imag) - product(gy_imag, gx_real)).astype(jnp.bfloat16)

    def marker_block(items):
        real_rows, imag_rows = items
        proj_real = product(real_rows, comm_real) - product(imag_rows, comm_imag)
        proj_imag = product(real_rows, comm_imag) + product(imag_rows, comm_real)
        return 2.0 * math.pi * jnp.sum(proj_imag * real_rows.astype(jnp.float32)
                                       - proj_real * imag_rows.astype(jnp.float32), axis=1)

    return lax.map(marker_block, (slab_real, slab_imag)).reshape(SITES)
```

```python
import functools
import math

import jax
import jax.numpy as jnp
from jax import lax
from jax.experimental import pallas as pl
from jax.experimental.pallas import tpu as pltpu
from jax.sharding import PartitionSpec as P

LX = 256
MESH = pl.DeviceIdType.MESH
TN = (((0,), (0,)), ((), ()))


def kernel(groups, panel_ref, cx_ref, cy_ref, out_ref, slab, acc, stage0, recv0, stage1, recv1,
           stage2, recv2, stage3, recv3, full, turned,
           local_sem, swap_send, swap_recv, pair_send, pair_recv, group_send, group_recv,
           gather_send, gather_recv, spread_send, spread_recv):
    rows, width = slab.shape[1], slab.shape[2]
    half = width // 2
    site, col = lax.axis_index("site"), lax.axis_index("col")
    core = site % 2
    pair = (site // 2) % 2
    group = site // 4
    other_core = (site + 1 - 2 * core, col)
    other_pair = (site + 2 - 4 * pair, col)
    other_col = (site, 1 - col)

    def peer(step):
        return (((group + step) % groups) * 4 + pair * 2 + core, col)

    barrier = pltpu.get_barrier_semaphore()
    for target in [other_core, other_pair, other_col] + [peer(d) for d in range(1, groups)]:
        pl.semaphore_signal(barrier, inc=1, device_id=target, device_id_type=MESH)
    pl.semaphore_wait(barrier, 3 + groups - 1)

    def send(src, dst, send_sem, recv_sem, target):
        copy = pltpu.make_async_remote_copy(
            src_ref=src, dst_ref=dst, send_sem=send_sem, recv_sem=recv_sem,
            device_id=target, device_id_type=MESH)
        copy.start()
        return copy

    pieces = 4
    tall = rows // pieces
    my_cols = pl.ds(pl.multiple_of(col * half, half), half)
    swaps, locals_ = [], []
    for k in range(pieces):
        there = pl.ds(pl.multiple_of((1 - col) * rows + k * tall, tall), tall)
        swaps.append(send(panel_ref.at[:, there, :], slab.at[:, pl.ds(k * tall, tall), my_cols],
                          swap_send.at[k], swap_recv.at[k], other_col))
    for k in range(pieces):
        here = pl.ds(pl.multiple_of(col * rows + k * tall, tall), tall)
        copy = pltpu.make_async_copy(
            panel_ref.at[:, here, :], slab.at[:, pl.ds(k * tall, tall), my_cols], local_sem.at[k])
        copy.start()
        locals_.append(copy)

    block = 256

    def gram(k, h):
        piece = pl.ds(k * tall, tall)
        weight = (cx_ref if h == 0 else cy_ref)[piece, :]

        @pl.loop(0, width // block)
        def _(j):
            at = pl.ds(pl.multiple_of(j * block, block), block)
            real = slab[0, piece, at].astype(jnp.float32)
            imag = slab[1, piece, at].astype(jnp.float32)
            first = (weight * (real + imag)).astype(jnp.bfloat16)
            second = (weight * (imag - real)).astype(jnp.bfloat16)
            part = lax.dot_general(first, slab[0, piece, :], TN, preferred_element_type=jnp.float32)
            part += lax.dot_general(second, slab[1, piece, :], TN, preferred_element_type=jnp.float32)
            if k == 0:
                acc[h, at, :] = part
            else:
                acc[h, at, :] += part

    step_rows = 64
    own = pl.ds(pl.multiple_of(core * half, half), half)
    away = pl.ds(pl.multiple_of((1 - core) * half, half), half)

    def aligned(start, size):
        return pl.ds(pl.multiple_of(start, 16), size)

    def begin0(h):
        @pl.loop(0, width // step_rows)
        def _(i):
            at = aligned(i * step_rows, step_rows)
            stage0[h, at, :] = acc[h, at, away].astype(jnp.bfloat16)
        return send(stage0.at[h], recv0.at[h], pair_send.at[0, h], pair_recv.at[0, h], other_core)

    halves = width // 2
    quarter = width // 4
    bits = [(col, pair), (pair, col)]
    targets = [(other_col, other_pair), (other_pair, other_col)]
    base1 = [bits[h][0] * halves for h in range(2)]
    base2 = [base1[h] + bits[h][1] * quarter for h in range(2)]
    chunk = quarter // groups
    base3 = [base2[h] + group * chunk for h in range(2)]

    def begin1(h):
        gone = (1 - bits[h][0]) * halves

        @pl.loop(0, halves // step_rows)
        def _(i):
            at = aligned(gone + i * step_rows, step_rows)
            stage1[h, aligned(i * step_rows, step_rows), :] = (
                acc[h, at, own] + recv0[h, at, :].astype(jnp.float32)).astype(jnp.bfloat16)
        copy = send(stage1.at[h], recv1.at[h], pair_send.at[1, h], pair_recv.at[1, h], targets[h][0])

        @pl.loop(0, halves // step_rows)
        def _(i):
            at = aligned(base1[h] + i * step_rows, step_rows)
            acc[h, at, own] += recv0[h, at, :].astype(jnp.float32)
        return copy

    def begin2(h):
        gone = (1 - bits[h][1]) * quarter
        kept = bits[h][1] * quarter

        @pl.loop(0, quarter // step_rows)
        def _(i):
            inner = aligned(gone + i * step_rows, step_rows)
            at = aligned(base1[h] + gone + i * step_rows, step_rows)
            stage2[h, aligned(i * step_rows, step_rows), :] = (
                acc[h, at, own] + recv1[h, inner, :].astype(jnp.float32)).astype(jnp.bfloat16)
        copy = send(stage2.at[h], recv2.at[h], pair_send.at[2, h], pair_recv.at[2, h], targets[h][1])

        @pl.loop(0, quarter // step_rows)
        def _(i):
            inner = aligned(kept + i * step_rows, step_rows)
            at = aligned(base2[h] + i * step_rows, step_rows)
            acc[h, at, own] += recv1[h, inner, :].astype(jnp.float32)
        return copy

    def begin3(h):
        @pl.loop(0, quarter // step_rows)
        def _(i):
            inner = aligned(i * step_rows, step_rows)
            at = aligned(base2[h] + i * step_rows, step_rows)
            total = acc[h, at, own] + recv2[h, inner, :].astype(jnp.float32)
            acc[h, at, own] = total
            stage3[h, inner, :] = total.astype(jnp.bfloat16)
        copies = []
        for d in range(1, groups):
            to = (group + d) % groups
            copies.append(send(stage3.at[h, aligned(to * chunk, chunk), :], recv3.at[h, d - 1],
                               group_send.at[h, d - 1], group_recv.at[h, d - 1], peer(d)))
        return copies

    def spread(h, rows_at, cols_at, which, target):
        place = full.at[h, rows_at, cols_at]
        return send(place, place, spread_send.at[which, h], spread_recv.at[which, h], target)

    def begin4(h):
        at = aligned(base3[h], chunk)
        total = acc[h, at, own]
        for d in range(1, groups):
            total += recv3[h, d - 1].astype(jnp.float32)
        full[h, at, own] = total.astype(jnp.bfloat16)
        place = full.at[h, at, own]
        return [send(place, place, gather_send.at[h, d - 1], gather_recv.at[h, d - 1], peer(d))
                for d in range(1, groups)]

    def begin5(h):
        return spread(h, aligned(base2[h], quarter), own, 0, targets[h][1])

    def begin6(h):
        return spread(h, aligned(base1[h], halves), own, 1, targets[h][0])

    def begin7(h):
        return spread(h, pl.ds(0, width), own, 2, other_core)

    for k in range(pieces):
        locals_[k].wait()
        swaps[k].wait()
        if k < pieces - 1:
            gram(k, 0)
            gram(k, 1)
    flight = [None, None]
    for h in range(2):
        gram(pieces - 1, h)
        flight[h] = [begin0(h)]
    for begin in (begin1, begin2, begin3, begin4, begin5, begin6, begin7):
        for h in range(2):
            for copy in flight[h]:
                copy.wait()
            started = begin(h)
            flight[h] = started if isinstance(started, list) else [started]
    for h in range(2):
        for copy in flight[h]:
            copy.wait()

    deep = 256

    @pl.loop(0, width // block)
    def _(c):
        at = pl.ds(pl.multiple_of(c * block, block), block)
        for h in range(2):
            turned[h] = full[h, at, :].T

        @pl.loop(0, rows // deep)
        def _(r):
            here = pl.ds(pl.multiple_of(r * deep, deep), deep)
            real, imag = slab[0, here, :], slab[1, here, :]
            dot = functools.partial(jnp.dot, preferred_element_type=jnp.float32)
            ps, qs = [], []
            for h in range(2):
                straight = full[h, :, at]
                ps.append(dot(real, turned[h]) + dot(imag, straight))
                qs.append(dot(imag, turned[h]) - dot(real, straight))
            term = 2.0 * math.pi * jnp.sum(qs[0] * ps[1] - ps[0] * qs[1], axis=1, keepdims=True)

            @pl.when(c == 0)
            def _():
                out_ref[here, :] = term

            @pl.when(c > 0)
            def _():
                out_ref[here, :] += term


def shards(panel, xs, ys):
    rows = panel.shape[1] // lax.axis_size("col")
    width = panel.shape[2] * lax.axis_size("col")
    devices = lax.axis_size("site") * lax.axis_size("col")
    groups = lax.axis_size("site") // 4
    lat_y = rows * devices // LX
    centre_x = xs.astype(jnp.float32) - (LX - 1) / 2.0
    centre_y = ys.astype(jnp.float32) - (lat_y - 1) / 2.0
    half, quarter = width // 2, width // 4
    dma = pltpu.SemaphoreType.DMA
    vmem = pl.BlockSpec(memory_space=pltpu.VMEM)
    out = pl.pallas_call(
        functools.partial(kernel, groups),
        out_shape=jax.ShapeDtypeStruct((rows, 1), jnp.float32),
        in_specs=[pl.BlockSpec(memory_space=pl.ANY), vmem, vmem],
        out_specs=vmem,
        scratch_shapes=[
            pltpu.VMEM((2, rows, width), jnp.bfloat16),
            pltpu.VMEM((2, width, width), jnp.float32),
            pltpu.VMEM((2, width, half), jnp.bfloat16),
            pltpu.VMEM((2, width, half), jnp.bfloat16),
            pltpu.VMEM((2, half, half), jnp.bfloat16),
            pltpu.VMEM((2, half, half), jnp.bfloat16),
            pltpu.VMEM((2, quarter, half), jnp.bfloat16),
            pltpu.VMEM((2, quarter, half), jnp.bfloat16),
            pltpu.VMEM((2, quarter, half), jnp.bfloat16),
            pltpu.VMEM((2, groups - 1, quarter // groups, half), jnp.bfloat16),
            pltpu.VMEM((2, width, width), jnp.bfloat16),
            pltpu.VMEM((2, width, 256), jnp.bfloat16),
            dma((4,)),
            dma((4,)),
            dma((4,)),
            dma((3, 2)),
            dma((3, 2)),
            dma((2, groups - 1)),
            dma((2, groups - 1)),
            dma((2, groups - 1)),
            dma((2, groups - 1)),
            dma((3, 2)),
            dma((3, 2)),
        ],
        compiler_params=pltpu.CompilerParams(
            collective_id=0, has_side_effects=True, vmem_limit_bytes=50 * 1024 * 1024),
    )(panel, centre_x[:, None], centre_y[:, None])
    return out[:, 0]


def solution(mesh):
    placed = (P(None, "site", "col"), P(("site", "col")), P(("site", "col")))
    return jax.shard_map(
        shards, mesh=mesh, in_specs=placed, out_specs=P(("site", "col")), check_vma=False
    )
```

```python
import functools
import math

import jax
import jax.numpy as jnp
from jax import lax
from jax.experimental import pallas as pl
from jax.experimental.pallas import tpu as pltpu
from jax.sharding import PartitionSpec as P

LX = 256
MESH = pl.DeviceIdType.MESH
TN = (((0,), (0,)), ((), ()))
BLOCK = 256
PIECES = 4
STEP = 64


def kernel(groups, panel_ref, centre_ref, out_ref, mine, got, theirs, weights,
           dacc, dstage0, drecv0, dstage1, drecv1, dstage2, drecv2, dfull,
           acc, stage0, recv0, stage1, recv1, stage2, recv2, stage3, recv3, ofull, turned, pq,
           local_sem, centre_sem, swap_send, swap_recv,
           dpair_send, dpair_recv, dgroup_send, dgroup_recv, dgather_send, dgather_recv,
           dspread_send, dspread_recv,
           pair_send, pair_recv, group_send, group_recv,
           gather_send, gather_recv, spread_send, spread_recv):
    rows, half = got.shape[1], got.shape[2]
    width, part_cols = 2 * half, half // 2
    site, col = lax.axis_index("site"), lax.axis_index("col")
    core = site % 2
    pair = (site // 2) % 2
    group = site // 4
    other_core = (site + 1 - 2 * core, col)
    other_pair = (site + 2 - 4 * pair, col)
    other_col = (site, 1 - col)

    def peer(step):
        return (((group + step) % groups) * 4 + pair * 2 + core, col)

    barrier = pltpu.get_barrier_semaphore()
    for target in [other_core, other_pair, other_col] + [peer(d) for d in range(1, groups)]:
        pl.semaphore_signal(barrier, inc=1, device_id=target, device_id_type=MESH)
    pl.semaphore_wait(barrier, 3 + groups - 1)

    def send(src, dst, send_sem, recv_sem, target):
        copy = pltpu.make_async_remote_copy(
            src_ref=src, dst_ref=dst, send_sem=send_sem, recv_sem=recv_sem,
            device_id=target, device_id_type=MESH)
        copy.start()
        return copy

    def aligned(start, size):
        return pl.ds(pl.multiple_of(start, 16), size)

    def wide(start, size):
        return pl.ds(pl.multiple_of(start, 256), size)

    tall = rows // PIECES
    centres = send(centre_ref, theirs, centre_sem.at[0], centre_sem.at[1], other_col)
    swaps = []
    for k in range(PIECES):
        swaps.append(send(panel_ref.at[:, wide((1 - col) * rows + k * tall, tall), :],
                          got.at[:, pl.ds(k * tall, tall), :],
                          swap_send.at[k], swap_recv.at[k], other_col))
    locals_ = []
    for n, at in enumerate((wide(col * rows, rows), wide((1 - col) * rows, rows))):
        copy = pltpu.make_async_copy(panel_ref.at[:, at, :], mine.at[:, at, :], local_sem.at[n])
        copy.start()
        locals_.append(copy)

    def spread_weights(n, source):
        for h in range(2):
            for i in range(rows // 128):
                line = jnp.broadcast_to(source[h, i:i + 1, :], (128, 128))
                weights[h, n, i * 128:(i + 1) * 128, :] = line.T

    def scaled(ref, h, n, weight_rows, at, lanes):
        line = weights[h, n, weight_rows, :]
        weight = jnp.concatenate([line] * (BLOCK // 128), axis=1)
        real = ref[0, at, lanes].astype(jnp.float32)
        imag = ref[1, at, lanes].astype(jnp.float32)
        return ((weight * (real + imag)).astype(jnp.bfloat16),
                (weight * (imag - real)).astype(jnp.bfloat16))

    def gram(first, second, ref, at):
        part = lax.dot_general(first, ref[0, at, :], TN, preferred_element_type=jnp.float32)
        return part + lax.dot_general(second, ref[1, at, :], TN, preferred_element_type=jnp.float32)

    def near_gram(n):
        start = (col if n == 0 else 1 - col) * rows

        @pl.loop(0, half // BLOCK)
        def _(j):
            lanes = wide(j * BLOCK, BLOCK)
            for h in range(2):
                total = None
                for k in range(2):
                    span = rows // 2
                    at = wide(start + k * span, span)
                    first, second = scaled(mine, h, n, pl.ds(k * span, span), at, lanes)
                    part = gram(first, second, mine, at)
                    total = part if total is None else total + part
                if n == 0:
                    dacc[h, lanes, :] = total
                else:
                    dacc[h, lanes, :] += total

    def far_gram(k, h):
        mine_at, got_at = wide(col * rows + k * tall, tall), pl.ds(k * tall, tall)

        @pl.loop(0, half // BLOCK)
        def _(j):
            lanes = wide(j * BLOCK, BLOCK)
            for left, left_at, right, right_at, base in (
                    (mine, mine_at, got, got_at, col * half),
                    (got, got_at, mine, mine_at, (1 - col) * half)):
                first, second = scaled(left, h, 0, got_at, left_at, lanes)
                part = gram(first, second, right, right_at)
                place = wide(base + j * BLOCK, BLOCK)
                if k == 0:
                    acc[h, place, :] = part
                else:
                    acc[h, place, :] += part

    own = pl.ds(pl.multiple_of(core * part_cols, part_cols), part_cols)
    away = pl.ds(pl.multiple_of((1 - core) * part_cols, part_cols), part_cols)
    quarter = half // 2
    chunk = quarter // groups

    def strips(count, body):
        @pl.loop(0, count // STEP)
        def _(i):
            body(i * STEP)

    def d0():
        def body(i):
            at = aligned(i, STEP)
            for h in range(2):
                dstage0[h, at, :] = dacc[h, at, away].astype(jnp.bfloat16)
        strips(half, body)
        return [send(dstage0, drecv0, dpair_send.at[0], dpair_recv.at[0], other_core)]

    def d1():
        def gone(i):
            at = aligned((1 - pair) * quarter + i, STEP)
            for h in range(2):
                dstage1[h, aligned(i, STEP), :] = (
                    dacc[h, at, own] + drecv0[h, at, :].astype(jnp.float32)).astype(jnp.bfloat16)

        def kept(i):
            at = aligned(pair * quarter + i, STEP)
            for h in range(2):
                dacc[h, at, own] += drecv0[h, at, :].astype(jnp.float32)
        strips(quarter, gone)
        copy = send(dstage1, drecv1, dpair_send.at[1], dpair_recv.at[1], other_pair)
        strips(quarter, kept)
        return [copy]

    def d2():
        def body(i):
            at, inner = aligned(pair * quarter + i, STEP), aligned(i, STEP)
            for h in range(2):
                total = dacc[h, at, own] + drecv1[h, inner, :].astype(jnp.float32)
                dacc[h, at, own] = total
                dstage2[h, inner, :] = total.astype(jnp.bfloat16)
        strips(quarter, body)
        copies = []
        for d in range(1, groups):
            to = (group + d) % groups
            copies.append(send(dstage2.at[:, aligned(to * chunk, chunk), :], drecv2.at[:, d - 1],
                               dgroup_send.at[d - 1], dgroup_recv.at[d - 1], peer(d)))
        return copies

    def dgather(n, which):
        place = dfull.at[:, aligned(which * half + pair * quarter + group * chunk, chunk), own]
        return [send(place, place, dgather_send.at[n, d - 1], dgather_recv.at[n, d - 1], peer(d))
                for d in range(1, groups)]

    def d3():
        at = aligned(pair * quarter + group * chunk, chunk)
        place = aligned(col * half + pair * quarter + group * chunk, chunk)
        for h in range(2):
            total = dacc[h, at, own]
            for d in range(1, groups):
                total += drecv2[h, d - 1].astype(jnp.float32)
            dfull[h, place, own] = total.astype(jnp.bfloat16)
        ref = dfull.at[:, place, own]
        return [send(ref, ref, dspread_send.at[0], dspread_recv.at[0], other_col)], dgather(0, col)

    def d5():
        copies = []
        for n, which in enumerate((col, 1 - col)):
            ref = dfull.at[:, wide(which * half + pair * quarter, quarter), own]
            copies.append(send(ref, ref, dspread_send.at[1 + n], dspread_recv.at[1 + n], other_pair))
        return copies

    def d6():
        ref = dfull.at[:, :, own]
        return [send(ref, ref, dspread_send.at[3], dspread_recv.at[3], other_core)]

    bits = [(col, pair), (pair, col)]
    targets = [(other_col, other_pair), (other_pair, other_col)]
    base1 = [bits[h][0] * half for h in range(2)]
    base2 = [base1[h] + bits[h][1] * quarter for h in range(2)]
    base3 = [base2[h] + group * chunk for h in range(2)]

    def o0(h):
        def body(i):
            at = aligned(i, STEP)
            stage0[h, at, :] = acc[h, at, away].astype(jnp.bfloat16)
        strips(width, body)
        return [send(stage0.at[h], recv0.at[h], pair_send.at[0, h], pair_recv.at[0, h], other_core)]

    def o1(h):
        def gone(i):
            at = aligned((1 - bits[h][0]) * half + i, STEP)
            stage1[h, aligned(i, STEP), :] = (
                acc[h, at, own] + recv0[h, at, :].astype(jnp.float32)).astype(jnp.bfloat16)

        def kept(i):
            at = aligned(base1[h] + i, STEP)
            acc[h, at, own] += recv0[h, at, :].astype(jnp.float32)
        strips(half, gone)
        copy = send(stage1.at[h], recv1.at[h], pair_send.at[1, h], pair_recv.at[1, h], targets[h][0])
        strips(half, kept)
        return [copy]

    def o2(h):
        def gone(i):
            inner = aligned((1 - bits[h][1]) * quarter + i, STEP)
            at = aligned(base1[h] + (1 - bits[h][1]) * quarter + i, STEP)
            stage2[h, aligned(i, STEP), :] = (
                acc[h, at, own] + recv1[h, inner, :].astype(jnp.float32)).astype(jnp.bfloat16)

        def kept(i):
            inner = aligned(bits[h][1] * quarter + i, STEP)
            at = aligned(base2[h] + i, STEP)
            acc[h, at, own] += recv1[h, inner, :].astype(jnp.float32)
        strips(quarter, gone)
        copy = send(stage2.at[h], recv2.at[h], pair_send.at[2, h], pair_recv.at[2, h], targets[h][1])
        strips(quarter, kept)
        return [copy]

    def o3(h):
        def body(i):
            inner, at = aligned(i, STEP), aligned(base2[h] + i, STEP)
            total = acc[h, at, own] + recv2[h, inner, :].astype(jnp.float32)
            acc[h, at, own] = total
            stage3[h, inner, :] = total.astype(jnp.bfloat16)
        strips(quarter, body)
        copies = []
        for d in range(1, groups):
            to = (group + d) % groups
            copies.append(send(stage3.at[h, aligned(to * chunk, chunk), :], recv3.at[h, d - 1],
                               group_send.at[h, d - 1], group_recv.at[h, d - 1], peer(d)))
        return copies

    def o4(h):
        at = aligned(base3[h], chunk)
        total = acc[h, at, own]
        for d in range(1, groups):
            total += recv3[h, d - 1].astype(jnp.float32)
        ofull[h, at, own] = total.astype(jnp.bfloat16)
        place = ofull.at[h, at, own]
        return [send(place, place, gather_send.at[h, d - 1], gather_recv.at[h, d - 1], peer(d))
                for d in range(1, groups)]

    def spread(h, at, which, target):
        place = ofull.at[h, at, own]
        return [send(place, place, spread_send.at[which, h], spread_recv.at[which, h], target)]

    def o5(h):
        return spread(h, wide(base2[h], quarter), 0, targets[h][1])

    def o6(h):
        return spread(h, wide(base1[h], half), 1, targets[h][0])

    def o7(h):
        return spread(h, pl.ds(0, width), 2, other_core)

    dot = functools.partial(jnp.dot, preferred_element_type=jnp.float32)
    deep = 256

    def project_near(side, j):
        which = col if side == 0 else 1 - col
        lanes = pl.ds(j * BLOCK, BLOCK)
        for h in range(2):
            turned[h] = dfull[h, wide(which * half + j * BLOCK, BLOCK), :].T

        @pl.loop(0, rows // deep)
        def _(r):
            here = wide(r * deep, deep)
            if side == 0:
                at = wide(col * rows + r * deep, deep)
                real, imag = mine[0, at, :], mine[1, at, :]
            else:
                real, imag = got[0, here, :], got[1, here, :]
            for h in range(2):
                straight = dfull[h, wide(which * half, half), lanes]
                pq[h, side, here, lanes] = dot(real, turned[h]) + dot(imag, straight)
                pq[2 + h, side, here, lanes] = dot(imag, turned[h]) - dot(real, straight)

    def project_far(side, j):
        which = col if side == 0 else 1 - col
        lanes = pl.ds(j * BLOCK, BLOCK)
        for h in range(2):
            turned[h] = ofull[h, wide(which * half + j * BLOCK, BLOCK), :].T

        @pl.loop(0, rows // deep)
        def _(r):
            here = wide(r * deep, deep)
            if side == 1:
                at = wide(col * rows + r * deep, deep)
                real, imag = mine[0, at, :], mine[1, at, :]
            else:
                real, imag = got[0, here, :], got[1, here, :]
            ps, qs = [], []
            for h in range(2):
                straight = ofull[h, wide((1 - which) * half, half), lanes]
                ps.append(pq[h, side, here, lanes] + dot(real, turned[h]) + dot(imag, straight))
                qs.append(pq[2 + h, side, here, lanes] + dot(imag, turned[h]) - dot(real, straight))
            term = 2.0 * math.pi * jnp.sum(qs[0] * ps[1] - ps[0] * qs[1], axis=1, keepdims=True)
            if side == 0 and j == 0:
                out_ref[here, :] = term
            else:
                out_ref[here, :] += term

    def finish(copies):
        for copy in copies:
            copy.wait()

    spread_weights(0, centre_ref)
    locals_[0].wait()
    near_gram(0)
    centres.wait()
    spread_weights(1, theirs)
    locals_[1].wait()
    near_gram(1)
    moving = d0()
    finish(moving)
    moving = d1()
    finish(moving)
    moving = d2()
    swaps[0].wait()
    far_gram(0, 0)
    far_gram(0, 1)
    finish(moving)
    across, around = d3()
    swaps[1].wait()
    far_gram(1, 0)
    far_gram(1, 1)
    finish(across)
    around2 = dgather(1, 1 - col)
    finish(around)
    swaps[2].wait()
    far_gram(2, 0)
    far_gram(2, 1)
    finish(around2)
    moving = d5()
    swaps[3].wait()
    flight = [None, None]
    for h in range(2):
        far_gram(3, h)
        flight[h] = o0(h)
    finish(moving)
    moving = d6()

    def advance(begin):
        for h in range(2):
            finish(flight[h])
            flight[h] = begin(h)

    advance(o1)
    finish(moving)
    project_near(0, 0)
    advance(o2)
    project_near(0, 1)
    advance(o3)
    advance(o4)
    advance(o5)
    project_near(1, 0)
    advance(o6)
    project_near(1, 1)
    advance(o7)
    for h in range(2):
        finish(flight[h])
    for side in range(2):
        for j in range(half // BLOCK):
            project_far(side, j)


def shards(panel, xs, ys):
    rows = panel.shape[1] // lax.axis_size("col")
    half = panel.shape[2]
    width = half * lax.axis_size("col")
    devices = lax.axis_size("site") * lax.axis_size("col")
    groups = lax.axis_size("site") // 4
    lat_y = rows * devices // LX
    centre_x = xs.astype(jnp.float32) - (LX - 1) / 2.0
    centre_y = ys.astype(jnp.float32) - (lat_y - 1) / 2.0
    centre = jnp.stack([centre_x, centre_y]).reshape(2, rows // 128, 128)
    quarter = half // 2
    chunk = quarter // groups
    dma = pltpu.SemaphoreType.DMA
    b16, f32 = jnp.bfloat16, jnp.float32
    vmem = pl.BlockSpec(memory_space=pltpu.VMEM)
    out = pl.pallas_call(
        functools.partial(kernel, groups),
        out_shape=jax.ShapeDtypeStruct((rows, 1), f32),
        in_specs=[pl.BlockSpec(memory_space=pl.ANY), vmem],
        out_specs=vmem,
        scratch_shapes=[
            pltpu.VMEM((2, 2 * rows, half), b16),
            pltpu.VMEM((2, rows, half), b16),
            pltpu.VMEM((2, rows // 128, 128), f32),
            pltpu.VMEM((2, 2, rows, 128), f32),
            pltpu.VMEM((2, half, half), f32),
            pltpu.VMEM((2, half, quarter), b16),
            pltpu.VMEM((2, half, quarter), b16),
            pltpu.VMEM((2, quarter, quarter), b16),
            pltpu.VMEM((2, quarter, quarter), b16),
            pltpu.VMEM((2, quarter, quarter), b16),
            pltpu.VMEM((2, groups - 1, chunk, quarter), b16),
            pltpu.VMEM((2, width, half), b16),
            pltpu.VMEM((2, width, half), f32),
            pltpu.VMEM((2, width, quarter), b16),
            pltpu.VMEM((2, width, quarter), b16),
            pltpu.VMEM((2, half, quarter), b16),
            pltpu.VMEM((2, half, quarter), b16),
            pltpu.VMEM((2, quarter, quarter), b16),
            pltpu.VMEM((2, quarter, quarter), b16),
            pltpu.VMEM((2, quarter, quarter), b16),
            pltpu.VMEM((2, groups - 1, chunk, quarter), b16),
            pltpu.VMEM((2, width, half), b16),
            pltpu.VMEM((2, half, BLOCK), b16),
            pltpu.VMEM((4, 2, rows, half), f32),
            dma((2,)), dma((2,)), dma((PIECES,)), dma((PIECES,)),
            dma((2,)), dma((2,)), dma((groups - 1,)), dma((groups - 1,)),
            dma((2, groups - 1)), dma((2, groups - 1)), dma((4,)), dma((4,)),
            dma((3, 2)), dma((3, 2)), dma((2, groups - 1)), dma((2, groups - 1)),
            dma((2, groups - 1)), dma((2, groups - 1)), dma((3, 2)), dma((3, 2)),
        ],
        compiler_params=pltpu.CompilerParams(
            collective_id=0, has_side_effects=True, vmem_limit_bytes=56 * 1024 * 1024),
    )(panel, centre)
    return out[:, 0]


def solution(mesh):
    placed = (P(None, "site", "col"), P(("site", "col")), P(("site", "col")))
    return jax.shard_map(
        shards, mesh=mesh, in_specs=placed, out_specs=P(("site", "col")), check_vma=False
    )
```

```python
import functools
import math

import jax
import jax.numpy as jnp
from jax import lax
from jax.experimental import pallas as pl
from jax.experimental.pallas import tpu as pltpu
from jax.sharding import PartitionSpec as P

LX = 256
MESH = pl.DeviceIdType.MESH
TN = (((0,), (0,)), ((), ()))
BLOCK = 256
PIECES = 4
STEP = 64


def kernel(groups, panel_ref, centre_ref, out_ref, mine, got, theirs, weights,
           dacc, dstage0, drecv0, dstage1, drecv1, dstage2, drecv2, dfull,
           acc, stage0, recv0, stage1, recv1, stage2, recv2, stage3, recv3, ofull, turned, pq,
           local_sem, centre_sem, swap_send, swap_recv,
           dpair_send, dpair_recv, dgroup_send, dgroup_recv, dgather_send, dgather_recv,
           dspread_send, dspread_recv,
           pair_send, pair_recv, group_send, group_recv,
           gather_send, gather_recv, spread_send, spread_recv):
    rows, half = got.shape[1], got.shape[2]
    width, part_cols = 2 * half, half // 2
    site, col = lax.axis_index("site"), lax.axis_index("col")
    core = site % 2
    pair = (site // 2) % 2
    group = site // 4
    other_core = (site + 1 - 2 * core, col)
    other_pair = (site + 2 - 4 * pair, col)
    other_col = (site, 1 - col)

    def peer(step):
        return (((group + step) % groups) * 4 + pair * 2 + core, col)

    barrier = pltpu.get_barrier_semaphore()
    for target in [other_core, other_pair, other_col] + [peer(d) for d in range(1, groups)]:
        pl.semaphore_signal(barrier, inc=1, device_id=target, device_id_type=MESH)
    pl.semaphore_wait(barrier, 3 + groups - 1)

    def send(src, dst, send_sem, recv_sem, target):
        copy = pltpu.make_async_remote_copy(
            src_ref=src, dst_ref=dst, send_sem=send_sem, recv_sem=recv_sem,
            device_id=target, device_id_type=MESH)
        copy.start()
        return copy

    def aligned(start, size):
        return pl.ds(pl.multiple_of(start, 16), size)

    def wide(start, size):
        return pl.ds(pl.multiple_of(start, 256), size)

    tall = rows // PIECES
    centres = send(centre_ref, theirs, centre_sem.at[0], centre_sem.at[1], other_col)

    def swap(k):
        return send(panel_ref.at[:, wide((1 - col) * rows + k * tall, tall), :],
                    got.at[:, pl.ds(k * tall, tall), :],
                    swap_send.at[k], swap_recv.at[k], other_col)

    swaps = [swap(0), swap(1)]
    locals_ = []
    for n, at in enumerate((wide(col * rows, rows), wide((1 - col) * rows, rows))):
        copy = pltpu.make_async_copy(panel_ref.at[:, at, :], mine.at[:, at, :], local_sem.at[n])
        copy.start()
        locals_.append(copy)

    def spread_weights(n, source):
        for h in range(2):
            for i in range(rows // 128):
                line = jnp.broadcast_to(source[h, i:i + 1, :], (128, 128))
                weights[h, n, i * 128:(i + 1) * 128, :] = line.T

    def scaled(ref, h, n, weight_rows, at, lanes):
        line = weights[h, n, weight_rows, :]
        weight = jnp.concatenate([line] * (BLOCK // 128), axis=1)
        real = ref[0, at, lanes].astype(jnp.float32)
        imag = ref[1, at, lanes].astype(jnp.float32)
        return ((weight * (real + imag)).astype(jnp.bfloat16),
                (weight * (imag - real)).astype(jnp.bfloat16))

    def gram(first, second, ref, at):
        part = lax.dot_general(first, ref[0, at, :], TN, preferred_element_type=jnp.float32)
        return part + lax.dot_general(second, ref[1, at, :], TN, preferred_element_type=jnp.float32)

    def near_gram(n):
        start = (col if n == 0 else 1 - col) * rows

        @pl.loop(0, half // BLOCK)
        def _(j):
            lanes = wide(j * BLOCK, BLOCK)
            for h in range(2):
                total = None
                for k in range(2):
                    span = rows // 2
                    at = wide(start + k * span, span)
                    first, second = scaled(mine, h, n, pl.ds(k * span, span), at, lanes)
                    part = gram(first, second, mine, at)
                    total = part if total is None else total + part
                if n == 0:
                    dacc[h, lanes, :] = total
                else:
                    dacc[h, lanes, :] += total

    def far_gram(k, h):
        mine_at, got_at = wide(col * rows + k * tall, tall), pl.ds(k * tall, tall)

        @pl.loop(0, half // BLOCK)
        def _(j):
            lanes = wide(j * BLOCK, BLOCK)
            for left, left_at, right, right_at, base in (
                    (mine, mine_at, got, got_at, col * half),
                    (got, got_at, mine, mine_at, (1 - col) * half)):
                first, second = scaled(left, h, 0, got_at, left_at, lanes)
                part = gram(first, second, right, right_at)
                place = wide(base + j * BLOCK, BLOCK)
                if k == 0:
                    acc[h, place, :] = part
                else:
                    acc[h, place, :] += part

    own = pl.ds(pl.multiple_of(core * part_cols, part_cols), part_cols)
    away = pl.ds(pl.multiple_of((1 - core) * part_cols, part_cols), part_cols)
    quarter = half // 2
    chunk = quarter // groups

    def strips(count, body):
        @pl.loop(0, count // STEP)
        def _(i):
            body(i * STEP)

    def d0():
        def body(i):
            at = aligned(i, STEP)
            for h in range(2):
                dstage0[h, at, :] = dacc[h, at, away].astype(jnp.bfloat16)
        strips(half, body)
        return [send(dstage0, drecv0, dpair_send.at[0], dpair_recv.at[0], other_core)]

    def d1():
        def gone(i):
            at = aligned((1 - pair) * quarter + i, STEP)
            for h in range(2):
                dstage1[h, aligned(i, STEP), :] = (
                    dacc[h, at, own] + drecv0[h, at, :].astype(jnp.float32)).astype(jnp.bfloat16)

        def kept(i):
            at = aligned(pair * quarter + i, STEP)
            for h in range(2):
                dacc[h, at, own] += drecv0[h, at, :].astype(jnp.float32)
        strips(quarter, gone)
        copy = send(dstage1, drecv1, dpair_send.at[1], dpair_recv.at[1], other_pair)
        strips(quarter, kept)
        return [copy]

    def d2():
        def body(i):
            at, inner = aligned(pair * quarter + i, STEP), aligned(i, STEP)
            for h in range(2):
                total = dacc[h, at, own] + drecv1[h, inner, :].astype(jnp.float32)
                dacc[h, at, own] = total
                dstage2[h, inner, :] = total.astype(jnp.bfloat16)
        strips(quarter, body)
        copies = []
        for d in range(1, groups):
            to = (group + d) % groups
            copies.append(send(dstage2.at[:, aligned(to * chunk, chunk), :], drecv2.at[:, d - 1],
                               dgroup_send.at[d - 1], dgroup_recv.at[d - 1], peer(d)))
        return copies

    def dgather(n, which):
        place = dfull.at[:, aligned(which * half + pair * quarter + group * chunk, chunk), own]
        return [send(place, place, dgather_send.at[n, d - 1], dgather_recv.at[n, d - 1], peer(d))
                for d in range(1, groups)]

    def d3():
        at = aligned(pair * quarter + group * chunk, chunk)
        place = aligned(col * half + pair * quarter + group * chunk, chunk)
        for h in range(2):
            total = dacc[h, at, own]
            for d in range(1, groups):
                total += drecv2[h, d - 1].astype(jnp.float32)
            dfull[h, place, own] = total.astype(jnp.bfloat16)
        ref = dfull.at[:, place, own]
        return [send(ref, ref, dspread_send.at[0], dspread_recv.at[0], other_col)], dgather(0, col)

    def d5():
        copies = []
        for n, which in enumerate((col, 1 - col)):
            ref = dfull.at[:, wide(which * half + pair * quarter, quarter), own]
            copies.append(send(ref, ref, dspread_send.at[1 + n], dspread_recv.at[1 + n], other_pair))
        return copies

    def d6():
        ref = dfull.at[:, :, own]
        return [send(ref, ref, dspread_send.at[3], dspread_recv.at[3], other_core)]

    bits = [(col, pair), (pair, col)]
    targets = [(other_col, other_pair), (other_pair, other_col)]
    base1 = [bits[h][0] * half for h in range(2)]
    base2 = [base1[h] + bits[h][1] * quarter for h in range(2)]
    base3 = [base2[h] + group * chunk for h in range(2)]

    def o0(h):
        def body(i):
            at = aligned(i, STEP)
            stage0[h, at, :] = acc[h, at, away].astype(jnp.bfloat16)
        strips(width, body)
        return [send(stage0.at[h], recv0.at[h], pair_send.at[0, h], pair_recv.at[0, h], other_core)]

    def o1(h):
        def gone(i):
            at = aligned((1 - bits[h][0]) * half + i, STEP)
            stage1[h, aligned(i, STEP), :] = (
                acc[h, at, own] + recv0[h, at, :].astype(jnp.float32)).astype(jnp.bfloat16)

        def kept(i):
            at = aligned(base1[h] + i, STEP)
            acc[h, at, own] += recv0[h, at, :].astype(jnp.float32)
        strips(half, gone)
        copy = send(stage1.at[h], recv1.at[h], pair_send.at[1, h], pair_recv.at[1, h], targets[h][0])
        strips(half, kept)
        return [copy]

    def o2(h):
        def gone(i):
            inner = aligned((1 - bits[h][1]) * quarter + i, STEP)
            at = aligned(base1[h] + (1 - bits[h][1]) * quarter + i, STEP)
            stage2[h, aligned(i, STEP), :] = (
                acc[h, at, own] + recv1[h, inner, :].astype(jnp.float32)).astype(jnp.bfloat16)

        def kept(i):
            inner = aligned(bits[h][1] * quarter + i, STEP)
            at = aligned(base2[h] + i, STEP)
            acc[h, at, own] += recv1[h, inner, :].astype(jnp.float32)
        strips(quarter, gone)
        copy = send(stage2.at[h], recv2.at[h], pair_send.at[2, h], pair_recv.at[2, h], targets[h][1])
        strips(quarter, kept)
        return [copy]

    def o3(h):
        def body(i):
            inner, at = aligned(i, STEP), aligned(base2[h] + i, STEP)
            total = acc[h, at, own] + recv2[h, inner, :].astype(jnp.float32)
            acc[h, at, own] = total
            stage3[h, inner, :] = total.astype(jnp.bfloat16)
        strips(quarter, body)
        copies = []
        for d in range(1, groups):
            to = (group + d) % groups
            copies.append(send(stage3.at[h, aligned(to * chunk, chunk), :], recv3.at[h, d - 1],
                               group_send.at[h, d - 1], group_recv.at[h, d - 1], peer(d)))
        return copies

    def o4(h):
        at = aligned(base3[h], chunk)
        total = acc[h, at, own]
        for d in range(1, groups):
            total += recv3[h, d - 1].astype(jnp.float32)
        ofull[h, at, own] = total.astype(jnp.bfloat16)
        place = ofull.at[h, at, own]
        return [send(place, place, gather_send.at[h, d - 1], gather_recv.at[h, d - 1], peer(d))
                for d in range(1, groups)]

    def spread(h, at, which, target):
        place = ofull.at[h, at, own]
        return [send(place, place, spread_send.at[which, h], spread_recv.at[which, h], target)]

    def o5(h):
        return spread(h, wide(base2[h], quarter), 0, targets[h][1])

    def o6(h):
        return spread(h, wide(base1[h], half), 1, targets[h][0])

    def o7(h):
        return spread(h, pl.ds(0, width), 2, other_core)

    dot = functools.partial(jnp.dot, preferred_element_type=jnp.float32)
    deep = 256

    def project_near(side, j):
        which = col if side == 0 else 1 - col
        lanes = pl.ds(j * BLOCK, BLOCK)
        for h in range(2):
            turned[h] = dfull[h, wide(which * half + j * BLOCK, BLOCK), :].T

        @pl.loop(0, rows // deep)
        def _(r):
            here = wide(r * deep, deep)
            if side == 0:
                at = wide(col * rows + r * deep, deep)
                real, imag = mine[0, at, :], mine[1, at, :]
            else:
                real, imag = got[0, here, :], got[1, here, :]
            for h in range(2):
                straight = dfull[h, wide(which * half, half), lanes]
                pq[h, side, here, lanes] = dot(real, turned[h]) + dot(imag, straight)
                pq[2 + h, side, here, lanes] = dot(imag, turned[h]) - dot(real, straight)

    def project_far(side, j):
        which = col if side == 0 else 1 - col
        lanes = pl.ds(j * BLOCK, BLOCK)
        for h in range(2):
            turned[h] = ofull[h, wide(which * half + j * BLOCK, BLOCK), :].T

        @pl.loop(0, rows // deep)
        def _(r):
            here = wide(r * deep, deep)
            if side == 1:
                at = wide(col * rows + r * deep, deep)
                real, imag = mine[0, at, :], mine[1, at, :]
            else:
                real, imag = got[0, here, :], got[1, here, :]
            ps, qs = [], []
            for h in range(2):
                straight = ofull[h, wide((1 - which) * half, half), lanes]
                ps.append(pq[h, side, here, lanes] + dot(real, turned[h]) + dot(imag, straight))
                qs.append(pq[2 + h, side, here, lanes] + dot(imag, turned[h]) - dot(real, straight))
            term = 2.0 * math.pi * jnp.sum(qs[0] * ps[1] - ps[0] * qs[1], axis=1, keepdims=True)
            if side == 0 and j == 0:
                out_ref[here, :] = term
            else:
                out_ref[here, :] += term

    def finish(copies):
        for copy in copies:
            copy.wait()

    spread_weights(0, centre_ref)
    locals_[0].wait()
    near_gram(0)
    centres.wait()
    spread_weights(1, theirs)
    locals_[1].wait()
    near_gram(1)
    moving = d0()
    finish(moving)
    moving = d1()
    finish(moving)
    moving = d2()
    swaps.append(swap(2))
    swaps[0].wait()
    far_gram(0, 0)
    far_gram(0, 1)
    finish(moving)
    across, around = d3()
    swaps.append(swap(3))
    swaps[1].wait()
    far_gram(1, 0)
    far_gram(1, 1)
    finish(across)
    around2 = dgather(1, 1 - col)
    finish(around)
    swaps[2].wait()
    far_gram(2, 0)
    far_gram(2, 1)
    finish(around2)
    moving = d5()
    swaps[3].wait()
    flight = [None, None]
    for h in range(2):
        far_gram(3, h)
        flight[h] = o0(h)

    def advance(begin):
        for h in range(2):
            finish(flight[h])
            flight[h] = begin(h)

    advance(o1)
    finish(moving)
    moving = d6()
    advance(o2)
    advance(o3)
    finish(moving)
    project_near(0, 0)
    advance(o4)
    project_near(0, 1)
    advance(o5)
    project_near(1, 0)
    advance(o6)
    project_near(1, 1)
    advance(o7)
    for h in range(2):
        finish(flight[h])
    for side in range(2):
        for j in range(half // BLOCK):
            project_far(side, j)


def shards(panel, xs, ys):
    rows = panel.shape[1] // lax.axis_size("col")
    half = panel.shape[2]
    width = half * lax.axis_size("col")
    devices = lax.axis_size("site") * lax.axis_size("col")
    groups = lax.axis_size("site") // 4
    lat_y = rows * devices // LX
    centre_x = xs.astype(jnp.float32) - (LX - 1) / 2.0
    centre_y = ys.astype(jnp.float32) - (lat_y - 1) / 2.0
    centre = jnp.stack([centre_x, centre_y]).reshape(2, rows // 128, 128)
    quarter = half // 2
    chunk = quarter // groups
    dma = pltpu.SemaphoreType.DMA
    b16, f32 = jnp.bfloat16, jnp.float32
    vmem = pl.BlockSpec(memory_space=pltpu.VMEM)
    out = pl.pallas_call(
        functools.partial(kernel, groups),
        out_shape=jax.ShapeDtypeStruct((rows, 1), f32),
        in_specs=[pl.BlockSpec(memory_space=pl.ANY), vmem],
        out_specs=vmem,
        scratch_shapes=[
            pltpu.VMEM((2, 2 * rows, half), b16),
            pltpu.VMEM((2, rows, half), b16),
            pltpu.VMEM((2, rows // 128, 128), f32),
            pltpu.VMEM((2, 2, rows, 128), f32),
            pltpu.VMEM((2, half, half), f32),
            pltpu.VMEM((2, half, quarter), b16),
            pltpu.VMEM((2, half, quarter), b16),
            pltpu.VMEM((2, quarter, quarter), b16),
            pltpu.VMEM((2, quarter, quarter), b16),
            pltpu.VMEM((2, quarter, quarter), b16),
            pltpu.VMEM((2, groups - 1, chunk, quarter), b16),
            pltpu.VMEM((2, width, half), b16),
            pltpu.VMEM((2, width, half), f32),
            pltpu.VMEM((2, width, quarter), b16),
            pltpu.VMEM((2, width, quarter), b16),
            pltpu.VMEM((2, half, quarter), b16),
            pltpu.VMEM((2, half, quarter), b16),
            pltpu.VMEM((2, quarter, quarter), b16),
            pltpu.VMEM((2, quarter, quarter), b16),
            pltpu.VMEM((2, quarter, quarter), b16),
            pltpu.VMEM((2, groups - 1, chunk, quarter), b16),
            pltpu.VMEM((2, width, half), b16),
            pltpu.VMEM((2, half, BLOCK), b16),
            pltpu.VMEM((4, 2, rows, half), f32),
            dma((2,)), dma((2,)), dma((PIECES,)), dma((PIECES,)),
            dma((2,)), dma((2,)), dma((groups - 1,)), dma((groups - 1,)),
            dma((2, groups - 1)), dma((2, groups - 1)), dma((4,)), dma((4,)),
            dma((3, 2)), dma((3, 2)), dma((2, groups - 1)), dma((2, groups - 1)),
            dma((2, groups - 1)), dma((2, groups - 1)), dma((3, 2)), dma((3, 2)),
        ],
        compiler_params=pltpu.CompilerParams(
            collective_id=0, has_side_effects=True, vmem_limit_bytes=56 * 1024 * 1024),
    )(panel, centre)
    return out[:, 0]


def solution(mesh):
    placed = (P(None, "site", "col"), P(("site", "col")), P(("site", "col")))
    return jax.shard_map(
        shards, mesh=mesh, in_specs=placed, out_specs=P(("site", "col")), check_vma=False
    )
```

```python
import functools
import math

import jax
import jax.numpy as jnp
from jax import lax
from jax.experimental import pallas as pl
from jax.experimental.pallas import tpu as pltpu
from jax.sharding import PartitionSpec as P

LX = 256
MESH = pl.DeviceIdType.MESH
TN = (((0,), (0,)), ((), ()))
BLOCK = 256
GRAM = 512
PIECES = 4
STEP = 64


def kernel(groups, panel_ref, centre_ref, out_ref, mine, got, theirs, weights,
           dacc, dstage0, drecv0, dstage1, drecv1, dstage2, drecv2, dfull,
           acc, stage0, recv0, stage1, recv1, stage2, recv2, stage3, recv3, ofull, turned, pq,
           local_sem, centre_sem, swap_send, swap_recv,
           dpair_send, dpair_recv, dgroup_send, dgroup_recv, dgather_send, dgather_recv,
           dspread_send, dspread_recv,
           pair_send, pair_recv, group_send, group_recv,
           gather_send, gather_recv, spread_send, spread_recv):
    rows, half = got.shape[1], got.shape[2]
    width, part_cols = 2 * half, half // 2
    site, col = lax.axis_index("site"), lax.axis_index("col")
    core = site % 2
    pair = (site // 2) % 2
    group = site // 4
    other_core = (site + 1 - 2 * core, col)
    other_pair = (site + 2 - 4 * pair, col)
    other_col = (site, 1 - col)

    def peer(step):
        return (((group + step) % groups) * 4 + pair * 2 + core, col)

    barrier = pltpu.get_barrier_semaphore()
    for target in [other_core, other_pair, other_col] + [peer(d) for d in range(1, groups)]:
        pl.semaphore_signal(barrier, inc=1, device_id=target, device_id_type=MESH)
    pl.semaphore_wait(barrier, 3 + groups - 1)

    def send(src, dst, send_sem, recv_sem, target):
        copy = pltpu.make_async_remote_copy(
            src_ref=src, dst_ref=dst, send_sem=send_sem, recv_sem=recv_sem,
            device_id=target, device_id_type=MESH)
        copy.start()
        return copy

    def aligned(start, size):
        return pl.ds(pl.multiple_of(start, 16), size)

    def wide(start, size):
        return pl.ds(pl.multiple_of(start, 256), size)

    tall = rows // PIECES
    centres = send(centre_ref, theirs, centre_sem.at[0], centre_sem.at[1], other_col)

    def swap(k):
        return send(panel_ref.at[:, wide((1 - col) * rows + k * tall, tall), :],
                    got.at[:, pl.ds(k * tall, tall), :],
                    swap_send.at[k], swap_recv.at[k], other_col)

    swaps = [swap(0), swap(1)]
    locals_ = []
    for n, at in enumerate((wide(col * rows, rows), wide((1 - col) * rows, rows))):
        copy = pltpu.make_async_copy(panel_ref.at[:, at, :], mine.at[:, at, :], local_sem.at[n])
        copy.start()
        locals_.append(copy)

    def spread_weights(n, source):
        for h in range(2):
            for i in range(rows // 128):
                line = jnp.broadcast_to(source[h, i:i + 1, :], (128, 128))
                weights[h, n, i * 128:(i + 1) * 128, :] = line.T

    def scaled(ref, h, n, weight_rows, at, lanes):
        line = weights[h, n, weight_rows, :]
        weight = jnp.concatenate([line] * (GRAM // 128), axis=1)
        real = ref[0, at, lanes].astype(jnp.float32)
        imag = ref[1, at, lanes].astype(jnp.float32)
        return ((weight * (real + imag)).astype(jnp.bfloat16),
                (weight * (imag - real)).astype(jnp.bfloat16))

    def gram(first, second, ref, at):
        part = lax.dot_general(first, ref[0, at, :], TN, preferred_element_type=jnp.float32)
        return part + lax.dot_general(second, ref[1, at, :], TN, preferred_element_type=jnp.float32)

    def near_gram(n):
        start = (col if n == 0 else 1 - col) * rows

        @pl.loop(0, half // GRAM)
        def _(j):
            lanes = wide(j * GRAM, GRAM)
            for h in range(2):
                total = None
                for k in range(2):
                    span = rows // 2
                    at = wide(start + k * span, span)
                    first, second = scaled(mine, h, n, pl.ds(k * span, span), at, lanes)
                    part = gram(first, second, mine, at)
                    total = part if total is None else total + part
                if n == 0:
                    dacc[h, lanes, :] = total
                else:
                    dacc[h, lanes, :] += total

    def far_gram(k, h):
        mine_at, got_at = wide(col * rows + k * tall, tall), pl.ds(k * tall, tall)

        @pl.loop(0, half // GRAM)
        def _(j):
            lanes = wide(j * GRAM, GRAM)
            for left, left_at, right, right_at, base in (
                    (mine, mine_at, got, got_at, col * half),
                    (got, got_at, mine, mine_at, (1 - col) * half)):
                first, second = scaled(left, h, 0, got_at, left_at, lanes)
                part = gram(first, second, right, right_at)
                place = wide(base + j * GRAM, GRAM)
                if k == 0:
                    acc[h, place, :] = part
                else:
                    acc[h, place, :] += part

    own = pl.ds(pl.multiple_of(core * part_cols, part_cols), part_cols)
    away = pl.ds(pl.multiple_of((1 - core) * part_cols, part_cols), part_cols)
    quarter = half // 2
    chunk = quarter // groups

    def strips(count, body):
        @pl.loop(0, count // STEP)
        def _(i):
            body(i * STEP)

    def d0():
        def body(i):
            at = aligned(i, STEP)
            for h in range(2):
                dstage0[h, at, :] = dacc[h, at, away].astype(jnp.bfloat16)
        strips(half, body)
        return [send(dstage0, drecv0, dpair_send.at[0], dpair_recv.at[0], other_core)]

    def d1():
        def gone(i):
            at = aligned((1 - pair) * quarter + i, STEP)
            for h in range(2):
                dstage1[h, aligned(i, STEP), :] = (
                    dacc[h, at, own] + drecv0[h, at, :].astype(jnp.float32)).astype(jnp.bfloat16)

        def kept(i):
            at = aligned(pair * quarter + i, STEP)
            for h in range(2):
                dacc[h, at, own] += drecv0[h, at, :].astype(jnp.float32)
        strips(quarter, gone)
        copy = send(dstage1, drecv1, dpair_send.at[1], dpair_recv.at[1], other_pair)
        strips(quarter, kept)
        return [copy]

    def d2():
        def body(i):
            at, inner = aligned(pair * quarter + i, STEP), aligned(i, STEP)
            for h in range(2):
                total = dacc[h, at, own] + drecv1[h, inner, :].astype(jnp.float32)
                dacc[h, at, own] = total
                dstage2[h, inner, :] = total.astype(jnp.bfloat16)
        strips(quarter, body)
        copies = []
        for d in range(1, groups):
            to = (group + d) % groups
            copies.append(send(dstage2.at[:, aligned(to * chunk, chunk), :], drecv2.at[:, d - 1],
                               dgroup_send.at[d - 1], dgroup_recv.at[d - 1], peer(d)))
        return copies

    def dgather(n, which):
        place = dfull.at[:, aligned(which * half + pair * quarter + group * chunk, chunk), own]
        return [send(place, place, dgather_send.at[n, d - 1], dgather_recv.at[n, d - 1], peer(d))
                for d in range(1, groups)]

    def d3():
        at = aligned(pair * quarter + group * chunk, chunk)
        place = aligned(col * half + pair * quarter + group * chunk, chunk)
        for h in range(2):
            total = dacc[h, at, own]
            for d in range(1, groups):
                total += drecv2[h, d - 1].astype(jnp.float32)
            dfull[h, place, own] = total.astype(jnp.bfloat16)
        ref = dfull.at[:, place, own]
        return [send(ref, ref, dspread_send.at[0], dspread_recv.at[0], other_col)], dgather(0, col)

    def d5():
        copies = []
        for n, which in enumerate((col, 1 - col)):
            ref = dfull.at[:, wide(which * half + pair * quarter, quarter), own]
            copies.append(send(ref, ref, dspread_send.at[1 + n], dspread_recv.at[1 + n], other_pair))
        return copies

    def d6():
        ref = dfull.at[:, :, own]
        return [send(ref, ref, dspread_send.at[3], dspread_recv.at[3], other_core)]

    bits = [(col, pair), (pair, col)]
    targets = [(other_col, other_pair), (other_pair, other_col)]
    base1 = [bits[h][0] * half for h in range(2)]
    base2 = [base1[h] + bits[h][1] * quarter for h in range(2)]
    base3 = [base2[h] + group * chunk for h in range(2)]

    def o0(h):
        def body(i):
            at = aligned(i, STEP)
            stage0[h, at, :] = acc[h, at, away].astype(jnp.bfloat16)
        strips(width, body)
        return [send(stage0.at[h], recv0.at[h], pair_send.at[0, h], pair_recv.at[0, h], other_core)]

    def o1(h):
        def gone(i):
            at = aligned((1 - bits[h][0]) * half + i, STEP)
            stage1[h, aligned(i, STEP), :] = (
                acc[h, at, own] + recv0[h, at, :].astype(jnp.float32)).astype(jnp.bfloat16)

        def kept(i):
            at = aligned(base1[h] + i, STEP)
            acc[h, at, own] += recv0[h, at, :].astype(jnp.float32)
        strips(half, gone)
        copy = send(stage1.at[h], recv1.at[h], pair_send.at[1, h], pair_recv.at[1, h], targets[h][0])
        strips(half, kept)
        return [copy]

    def o2(h):
        def gone(i):
            inner = aligned((1 - bits[h][1]) * quarter + i, STEP)
            at = aligned(base1[h] + (1 - bits[h][1]) * quarter + i, STEP)
            stage2[h, aligned(i, STEP), :] = (
                acc[h, at, own] + recv1[h, inner, :].astype(jnp.float32)).astype(jnp.bfloat16)

        def kept(i):
            inner = aligned(bits[h][1] * quarter + i, STEP)
            at = aligned(base2[h] + i, STEP)
            acc[h, at, own] += recv1[h, inner, :].astype(jnp.float32)
        strips(quarter, gone)
        copy = send(stage2.at[h], recv2.at[h], pair_send.at[2, h], pair_recv.at[2, h], targets[h][1])
        strips(quarter, kept)
        return [copy]

    def o3(h):
        def body(i):
            inner, at = aligned(i, STEP), aligned(base2[h] + i, STEP)
            total = acc[h, at, own] + recv2[h, inner, :].astype(jnp.float32)
            acc[h, at, own] = total
            stage3[h, inner, :] = total.astype(jnp.bfloat16)
        strips(quarter, body)
        copies = []
        for d in range(1, groups):
            to = (group + d) % groups
            copies.append(send(stage3.at[h, aligned(to * chunk, chunk), :], recv3.at[h, d - 1],
                               group_send.at[h, d - 1], group_recv.at[h, d - 1], peer(d)))
        return copies

    def o4(h):
        at = aligned(base3[h], chunk)
        total = acc[h, at, own]
        for d in range(1, groups):
            total += recv3[h, d - 1].astype(jnp.float32)
        ofull[h, at, own] = total.astype(jnp.bfloat16)
        place = ofull.at[h, at, own]
        return [send(place, place, gather_send.at[h, d - 1], gather_recv.at[h, d - 1], peer(d))
                for d in range(1, groups)]

    def spread(h, at, which, target):
        place = ofull.at[h, at, own]
        return [send(place, place, spread_send.at[which, h], spread_recv.at[which, h], target)]

    def o5(h):
        return spread(h, wide(base2[h], quarter), 0, targets[h][1])

    def o6(h):
        return spread(h, wide(base1[h], half), 1, targets[h][0])

    def o7(h):
        return spread(h, pl.ds(0, width), 2, other_core)

    dot = functools.partial(jnp.dot, preferred_element_type=jnp.float32)
    deep = 512

    def project_near(side, j):
        which = col if side == 0 else 1 - col
        lanes = pl.ds(j * BLOCK, BLOCK)
        for h in range(2):
            turned[h] = dfull[h, wide(which * half + j * BLOCK, BLOCK), :].T

        @pl.loop(0, rows // deep)
        def _(r):
            here = wide(r * deep, deep)
            if side == 0:
                at = wide(col * rows + r * deep, deep)
                real, imag = mine[0, at, :], mine[1, at, :]
            else:
                real, imag = got[0, here, :], got[1, here, :]
            for h in range(2):
                straight = dfull[h, wide(which * half, half), lanes]
                pq[h, side, here, lanes] = dot(real, turned[h]) + dot(imag, straight)
                pq[2 + h, side, here, lanes] = dot(imag, turned[h]) - dot(real, straight)

    def project_far(side, j):
        which = col if side == 0 else 1 - col
        lanes = pl.ds(j * BLOCK, BLOCK)
        for h in range(2):
            turned[h] = ofull[h, wide(which * half + j * BLOCK, BLOCK), :].T

        @pl.loop(0, rows // deep)
        def _(r):
            here = wide(r * deep, deep)
            if side == 1:
                at = wide(col * rows + r * deep, deep)
                real, imag = mine[0, at, :], mine[1, at, :]
            else:
                real, imag = got[0, here, :], got[1, here, :]
            ps, qs = [], []
            for h in range(2):
                straight = ofull[h, wide((1 - which) * half, half), lanes]
                ps.append(pq[h, side, here, lanes] + dot(real, turned[h]) + dot(imag, straight))
                qs.append(pq[2 + h, side, here, lanes] + dot(imag, turned[h]) - dot(real, straight))
            term = 2.0 * math.pi * jnp.sum(qs[0] * ps[1] - ps[0] * qs[1], axis=1, keepdims=True)
            if side == 0 and j == 0:
                out_ref[here, :] = term
            else:
                out_ref[here, :] += term

    def finish(copies):
        for copy in copies:
            copy.wait()

    spread_weights(0, centre_ref)
    locals_[0].wait()
    near_gram(0)
    centres.wait()
    spread_weights(1, theirs)
    locals_[1].wait()
    near_gram(1)
    moving = d0()
    finish(moving)
    moving = d1()
    finish(moving)
    moving = d2()
    swaps.append(swap(2))
    swaps[0].wait()
    far_gram(0, 0)
    far_gram(0, 1)
    finish(moving)
    across, around = d3()
    swaps.append(swap(3))
    swaps[1].wait()
    far_gram(1, 0)
    far_gram(1, 1)
    finish(across)
    around2 = dgather(1, 1 - col)
    finish(around)
    swaps[2].wait()
    far_gram(2, 0)
    far_gram(2, 1)
    finish(around2)
    moving = d5()
    swaps[3].wait()
    flight = [None, None]
    for h in range(2):
        far_gram(3, h)
        flight[h] = o0(h)

    def advance(begin):
        for h in range(2):
            finish(flight[h])
            flight[h] = begin(h)

    advance(o1)
    finish(moving)
    moving = d6()
    advance(o2)
    advance(o3)
    finish(moving)
    project_near(0, 0)
    advance(o4)
    project_near(0, 1)
    advance(o5)
    project_near(1, 0)
    advance(o6)
    project_near(1, 1)
    advance(o7)
    for h in range(2):
        finish(flight[h])
    for side in range(2):
        for j in range(half // BLOCK):
            project_far(side, j)


def shards(panel, xs, ys):
    rows = panel.shape[1] // lax.axis_size("col")
    half = panel.shape[2]
    width = half * lax.axis_size("col")
    devices = lax.axis_size("site") * lax.axis_size("col")
    groups = lax.axis_size("site") // 4
    lat_y = rows * devices // LX
    centre_x = xs.astype(jnp.float32) - (LX - 1) / 2.0
    centre_y = ys.astype(jnp.float32) - (lat_y - 1) / 2.0
    centre = jnp.stack([centre_x, centre_y]).reshape(2, rows // 128, 128)
    quarter = half // 2
    chunk = quarter // groups
    dma = pltpu.SemaphoreType.DMA
    b16, f32 = jnp.bfloat16, jnp.float32
    vmem = pl.BlockSpec(memory_space=pltpu.VMEM)
    out = pl.pallas_call(
        functools.partial(kernel, groups),
        out_shape=jax.ShapeDtypeStruct((rows, 1), f32),
        in_specs=[pl.BlockSpec(memory_space=pl.ANY), vmem],
        out_specs=vmem,
        scratch_shapes=[
            pltpu.VMEM((2, 2 * rows, half), b16),
            pltpu.VMEM((2, rows, half), b16),
            pltpu.VMEM((2, rows // 128, 128), f32),
            pltpu.VMEM((2, 2, rows, 128), f32),
            pltpu.VMEM((2, half, half), f32),
            pltpu.VMEM((2, half, quarter), b16),
            pltpu.VMEM((2, half, quarter), b16),
            pltpu.VMEM((2, quarter, quarter), b16),
            pltpu.VMEM((2, quarter, quarter), b16),
            pltpu.VMEM((2, quarter, quarter), b16),
            pltpu.VMEM((2, groups - 1, chunk, quarter), b16),
            pltpu.VMEM((2, width, half), b16),
            pltpu.VMEM((2, width, half), f32),
            pltpu.VMEM((2, width, quarter), b16),
            pltpu.VMEM((2, width, quarter), b16),
            pltpu.VMEM((2, half, quarter), b16),
            pltpu.VMEM((2, half, quarter), b16),
            pltpu.VMEM((2, quarter, quarter), b16),
            pltpu.VMEM((2, quarter, quarter), b16),
            pltpu.VMEM((2, quarter, quarter), b16),
            pltpu.VMEM((2, groups - 1, chunk, quarter), b16),
            pltpu.VMEM((2, width, half), b16),
            pltpu.VMEM((2, half, BLOCK), b16),
            pltpu.VMEM((4, 2, rows, half), f32),
            dma((2,)), dma((2,)), dma((PIECES,)), dma((PIECES,)),
            dma((2,)), dma((2,)), dma((groups - 1,)), dma((groups - 1,)),
            dma((2, groups - 1)), dma((2, groups - 1)), dma((4,)), dma((4,)),
            dma((3, 2)), dma((3, 2)), dma((2, groups - 1)), dma((2, groups - 1)),
            dma((2, groups - 1)), dma((2, groups - 1)), dma((3, 2)), dma((3, 2)),
        ],
        compiler_params=pltpu.CompilerParams(
            collective_id=0, has_side_effects=True, vmem_limit_bytes=56 * 1024 * 1024),
    )(panel, centre)
    return out[:, 0]


def solution(mesh):
    placed = (P(None, "site", "col"), P(("site", "col")), P(("site", "col")))
    return jax.shard_map(
        shards, mesh=mesh, in_specs=placed, out_specs=P(("site", "col")), check_vma=False
    )
```
